128 devices in a mesh: section: 4 (over x_hi, core), field: 4 (over y), dp: 8 (over x_lo, z).
Axes of the slice: x: 4 (x_hi: 2, x_lo: 2; x = x_hi * 2 + x_lo), y: 4, z: 4, core: 2. Of those that a mesh axis runs over, the one named last changes fastest.
Arguments:
- patches: bfloat16 [4, 1024, 8, 512], P(None, 'dp', 'field'), may hold values from -6 to 6
- field_mask: int32 [4, 1024, 8], P(None, 'dp', 'field'), may hold values 0 or 1
- order: int32 [4], replicated, may hold values from 0 to 3, each once
- embed_weight: bfloat16 [8, 512, 4096], P('field'), may hold values from -0.09375 to 0.09375
- embed_bias: bfloat16 [8, 4096], P('field'), may hold values from -3 to 3
- norm_gain: float32 [4, 4096], P('section'), may hold values from 0.1 to 1.9
- w_up: bfloat16 [4, 4096, 5632], P('section', 'dp', 'field'), may hold values from -0.09375 to 0.09375
- w_down: bfloat16 [4, 5632, 4096], P('section', 'field', 'dp'), may hold values from -0.109375 to 0.109375
Outputs:
- hidden_out: bfloat16 [4, 1024, 4096], P('section', 'dp', 'field')
The draws below stay inside these ranges and needn't reach their ends.
Inputs may be any that keep to these rules, and one draw needn't show every extreme that they name: `order`: each micro-batch appears once.
All inputs are finite; a program needn't handle non-finite values. No bound on the sum of `field_mask` on one device may be relied on, other than what follows from the above.
Results may differ from the reference program's by a relative error of at most 0.03.
Values may be sent and summed in bfloat16 or wider, within the bound.
No kernel may reach another device: no remote copies, remote signals or barrier semaphores. Data moves between devices by JAX's collectives and lax.ppermute only.
A program may use at most 128 MiB of HBM per device.

```python
import jax
import jax.numpy as jnp
from jax import lax

D = 4096
FFW = 5632
PATCH = 512
FIELDS = 8
MICRO = 4
LAYERS = 4
MB = 1024
N_FIELD = 4


def with_ends(drawn, own_key, low, high):
    extent = drawn.shape
    spot = [jax.random.randint(jax.random.fold_in(own_key, axis), (), 0, extent[axis]) for axis in range(len(extent))]
    drawn = drawn.at[tuple(spot)].set(low)
    longest = extent.index(max(extent))
    spot[longest] = (spot[longest] + 1) % extent[longest]
    return drawn.at[tuple(spot)].set(high)


def with_spikes(entries, key, source, target, parts, factor):
    owner, partner = [(jnp.arange(entries.shape[dim]) // (entries.shape[dim] // parts)).reshape([-1 if axis == dim else 1 for axis in range(entries.ndim)]) for dim in (source, target)]
    chosen = jax.random.permutation(key, parts)[partner]
    strong = (owner == chosen) | (owner == (partner + parts // 2) % parts)
    return jnp.where(strong, factor * entries, entries)


def level_of(own_key, shape, cuts, least, high):
    loudness = 1.0
    for dim, shards_of in cuts:
        draws = jax.random.uniform(jax.random.fold_in(jax.random.fold_in(own_key, 6), dim), (shards_of,), jnp.float32, least / len(cuts), high / len(cuts))
        loudness = loudness * jnp.repeat(jnp.exp(draws), shape[dim] // shards_of).reshape((-1,) + (1,) * (len(shape) - 1 - dim))
    return loudness


def normal_values(key, shape, spread, bound, split=(), kind=jnp.bfloat16):
    values = jax.random.normal(key, shape, jnp.float32) * spread
    if len(split) > 0:
        values = level_of(key, shape, split, -0.22, 0.18) * values
    return jnp.clip(values, min=-bound, max=bound).astype(kind)


def gaussian_with(rng, dims, deviation, limit, pieces, heavy, kind=jnp.bfloat16):
    values = deviation * jax.random.normal(rng, dims, jnp.float32)
    if pieces:
        values = values * level_of(rng, dims, pieces, -0.22, 0.18)
    return jnp.clip(with_spikes(values, jax.random.fold_in(rng, 3), *heavy), -limit, limit).astype(kind)


def setup_inputs(seed: int = 0) -> dict:
    seeds = jax.random.split(jax.random.key(seed), 9)
    return {
        "patches": normal_values(seeds[0], (MICRO, MB, FIELDS, PATCH), 1.0, 6.0, ((1, 8), (2, 4))),
        "field_mask": with_ends((jax.random.randint(seeds[1], (MICRO, MB, FIELDS), 0, 4) < 3).astype(jnp.int32), jax.random.fold_in(seeds[1], 1), 0, 1),
        "order": jax.random.permutation(seeds[2], MICRO).astype(jnp.int32),
        "embed_weight": normal_values(seeds[3], (FIELDS, PATCH, D), (PATCH * FIELDS) ** -0.5, 0.09375, ((0, 4),)),
        "embed_bias": normal_values(seeds[4], (FIELDS, D), 0.5, 3.0, ((0, 4),)),
        "norm_gain": jnp.clip(1.0 + 0.18 * jax.random.normal(seeds[5], (LAYERS, D), jnp.float32), 0.1, 1.9),
        "w_up": normal_values(seeds[6], (LAYERS, D, FFW), D ** -0.5, 0.09375, ((0, 4), (1, 8), (2, 4))),
        "w_down": gaussian_with(seeds[7], (LAYERS, FFW, D), FFW ** -0.5, 0.109375, ((0, 4), (1, 4), (2, 8)), (1, 2, 8, 2.0)),
    }


def reference(patches, field_mask, order, embed_weight, embed_bias, norm_gain, w_up, w_down):
    group_fields = FIELDS // N_FIELD
    group_units = FFW // N_FIELD
    results = []
    for position in range(MICRO):
        chosen = order[position]
        piece = patches[chosen]
        present = field_mask[chosen]
        masked = piece * present.astype(jnp.bfloat16)[:, :, None]
        total = jnp.zeros((MB, D), jnp.float32)
        for group in range(N_FIELD):
            lower = group * group_fields
            upper = lower + group_fields
            term = jnp.einsum('tfp,fpd->td', masked[:, lower:upper].astype(jnp.float32), embed_weight[lower:upper].astype(jnp.float32))
            term = term + jnp.dot(present[:, lower:upper].astype(jnp.float32), embed_bias[lower:upper].astype(jnp.float32))
            total = total + lax.optimization_barrier(term.astype(jnp.bfloat16)).astype(jnp.float32)
        state = total.astype(jnp.bfloat16)
        for layer in range(LAYERS):
            values = state.astype(jnp.float32)
            scale = lax.rsqrt(lax.optimization_barrier(jnp.mean(values * values, axis=-1, keepdims=True)) + 1e-05)
            normed = (values * scale * norm_gain[layer][None, :]).astype(jnp.bfloat16)
            upward = jnp.dot(normed, w_up[layer], preferred_element_type=jnp.float32)
            active = jax.nn.gelu(upward, approximate=True).astype(jnp.bfloat16)
            summed = jnp.zeros((MB, D), jnp.float32)
            for group in range(N_FIELD):
                lower = group * group_units
                upper = lower + group_units
                part = jnp.dot(active[:, lower:upper], w_down[layer][lower:upper], preferred_element_type=jnp.float32)
                summed = summed + lax.optimization_barrier(part.astype(jnp.bfloat16)).astype(jnp.float32)
            state = (values + summed).astype(jnp.bfloat16)
        results.append(state)
    return jnp.stack(results)
```

```python
import jax
import jax.numpy as jnp
from jax import lax
from jax.experimental import pallas as pl
from jax.experimental.pallas import tpu as pltpu
from jax.sharding import Mesh, PartitionSpec as P

AXES = ("xh", "core", "y", "xl", "z")
SIZES = (2, 2, 4, 2, 4)
RING = 4
EPS = 1e-05
VMEM = pl.BlockSpec(memory_space=pltpu.VMEM)
SMEM = pl.BlockSpec(memory_space=pltpu.SMEM)


def call(kernel, out_shape, in_specs, scratch=(), flops=0, nbytes=0):
    return pl.pallas_call(
        kernel,
        out_shape=out_shape,
        in_specs=in_specs,
        out_specs=jax.tree.map(lambda _: VMEM, out_shape),
        scratch_shapes=list(scratch),
        compiler_params=pltpu.CompilerParams(vmem_limit_bytes=40 * 2**20),
        cost_estimate=pl.CostEstimate(flops=flops, bytes_accessed=nbytes, transcendentals=0),
    )


def embed_kernel(place, masked, present, weight, bias, *outs):
    core, y = place[0], place[1]
    half = 256
    piece = masked[...]
    for ahead in range(RING):
        block = lax.rem(y + ahead, RING)
        for xl in range(2):
            for rel in range(2):
                side = core if rel == 0 else 1 - core
                start = (block + RING * xl) * (2 * half) + side * half
                at = pl.ds(pl.multiple_of(start, half), half)
                total = jnp.dot(
                    piece, weight[:, at], preferred_element_type=jnp.float32
                )
                for f in range(2):
                    total += present[:, f : f + 1] * bias[f : f + 1, at].astype(jnp.float32)
                outs[ahead][:, pl.ds(xl * 2 * half + rel * half, half)] = total.astype(
                    jnp.bfloat16
                )


def up_kernel(place, x0, x1, x2, x3, own, other, *rest):
    outs, (held, made) = rest[:RING], rest[RING:]
    y, z = place[1], place[2]
    for behind, block in enumerate((x0, x1, x2, x3)):
        held[lax.rem(y + RING - behind, RING)] = block[...]
    rows = held.shape[0] * held.shape[1]
    hidden = own.shape[2]
    half = own.shape[1]
    x = held[...].reshape(rows, held.shape[2])
    for start in range(0, hidden, 256):
        wide = min(256, hidden - start)
        at = slice(start, start + wide)
        total = jnp.zeros((rows, wide), jnp.float32)
        for xl in range(2):
            for rel, part in enumerate((own, other)):
                k = (xl * 2 + rel) * half
                total += jnp.dot(
                    x[:, k : k + half], part[xl, :, at], preferred_element_type=jnp.float32
                )
        made[:, :, at] = total.astype(jnp.bfloat16).reshape(RING, rows // RING, wide)
    values = x.astype(jnp.float32)
    square = jnp.sum(values * values, axis=1, keepdims=True)
    high = square.astype(jnp.bfloat16).astype(jnp.float32)
    lane = lax.broadcasted_iota(jnp.int32, (rows, 128), 1)
    tail = jnp.where(lane == 0, high, jnp.where(lane == 1, square - high, 0.0))
    made[:, :, hidden:] = tail.astype(jnp.bfloat16).reshape(RING, rows // RING, 128)
    for ahead in range(RING):
        outs[ahead][...] = made[lax.rem(z + ahead, RING)]


def act_kernel(width, h0, h1, h2, h3, out):
    hidden = out.shape[1]
    blocks = (h0, h1, h2, h3)
    square = jnp.zeros((out.shape[0], 1), jnp.float32)
    for block in blocks:
        tail = block[:, hidden:].astype(jnp.float32)
        square += jnp.sum(tail, axis=1, keepdims=True)
    scale = lax.rsqrt(square / width + EPS)
    total = jnp.zeros(out.shape, jnp.float32)
    for block in blocks:
        total += block[:, :hidden].astype(jnp.float32)
    out[...] = jax.nn.gelu(total * scale, approximate=True).astype(jnp.bfloat16)


def down_kernel(place, a0, a1, a2, a3, own, other, *rest):
    outs, (held, made) = rest[:RING], rest[RING:]
    y, z = place[1], place[2]
    for behind, block in enumerate((a0, a1, a2, a3)):
        held[lax.rem(z + RING - behind, RING)] = block[...]
    rows = held.shape[0] * held.shape[1]
    half = own.shape[2]
    act = held[...].reshape(rows, held.shape[2])
    for xl in range(2):
        for rel, part in enumerate((own, other)):
            k = (xl * 2 + rel) * half
            total = jnp.dot(act, part[xl], preferred_element_type=jnp.float32)
            made[:, :, k : k + half] = total.astype(jnp.bfloat16).reshape(
                RING, rows // RING, half
            )
    for ahead in range(RING):
        outs[ahead][...] = made[lax.rem(y + ahead, RING)]


def to_ahead(block, axis, distance):
    return lax.ppermute(block, axis, [(i, (i + distance) % RING) for i in range(RING)])


def send_each(blocks, axis):
    moved = {d: to_ahead(blocks[d], axis, d) for d in (2, 1, 3)}
    return [blocks[0], moved[1], moved[2], moved[3]]


def gather_behind(block, axis):
    return send_each([block] * RING, axis)


def swap_core(block):
    return lax.ppermute(block, "core", [(0, 1), (1, 0)])


def grid_move(block, target):
    route = [
        (y * RING + z, target(y, z)[0] * RING + target(y, z)[1])
        for y in range(RING)
        for z in range(RING)
    ]
    return lax.ppermute(block, ("y", "z"), route)


def per_device(patches, field_mask, order, embed_weight, embed_bias, norm_gain, w_up, w_down):
    xh, core, y, xl, z = (lax.axis_index(name) for name in AXES)
    first = core == 0
    tokens = patches.shape[1]
    width = embed_weight.shape[2]
    rows_up = w_up.shape[1]
    hidden = w_up.shape[2]
    half = rows_up // 2
    narrow = width // RING
    place = jnp.stack([core, y, z]).astype(jnp.int32)

    gain = lax.dynamic_slice(norm_gain[0], ((xl * RING + z) * rows_up,), (rows_up,))
    up = (w_up[0].astype(jnp.float32) * gain[:, None]).astype(jnp.bfloat16)
    down = w_down[0]
    up_low, up_high = up[:half], up[half:]
    down_low, down_high = down[:, :half], down[:, half:]
    up_got = swap_core(jnp.where(first, up_high, up_low))
    down_got = swap_core(jnp.where(first, down_high, down_low))
    ups, downs = [], []
    for kind in range(2):
        for low, high, got, into in ((up_low, up_high, up_got, ups), (down_low, down_high, down_got, downs)):
            mine = jnp.where(first, low, got) if kind == 0 else jnp.where(first, got, high)
            own = lax.all_gather(mine, ("xh", "xl"), axis=0, tiled=False)
            into.append((own, swap_core(own)))

    chosen = order[2 * xh + core]
    piece = lax.dynamic_index_in_dim(patches, chosen, 0, keepdims=False)
    present = lax.dynamic_index_in_dim(field_mask, chosen, 0, keepdims=False)
    masked = (piece * present.astype(jnp.bfloat16)[:, :, None]).reshape(tokens, -1)
    block = jax.ShapeDtypeStruct((tokens, narrow), jnp.bfloat16)
    terms = call(
        embed_kernel,
        [block] * RING,
        [SMEM, VMEM, VMEM, VMEM, VMEM],
        flops=2 * tokens * masked.shape[1] * width,
        nbytes=2 * masked.shape[1] * width,
    )(
        place,
        masked,
        present.astype(jnp.float32),
        embed_weight.reshape(-1, width),
        embed_bias,
    )
    moved = [
        grid_move(terms[d], lambda a, b, d=d: (b, (a + d) % RING)) for d in range(RING)
    ]
    x = sum(t.astype(jnp.float32) for t in moved).astype(jnp.bfloat16)

    sent = jax.ShapeDtypeStruct((tokens, hidden + 128), jnp.bfloat16)
    acted = jax.ShapeDtypeStruct((tokens, hidden), jnp.bfloat16)
    product = 2 * RING * tokens * narrow * hidden
    for layer in range(4):
        pair = layer // 2
        up_own, up_other = (w[2 * pair : 2 * pair + 2] for w in ups[layer % 2])
        down_own, down_other = (w[2 * pair : 2 * pair + 2] for w in downs[layer % 2])
        parts = call(
            up_kernel,
            [sent] * RING,
            [SMEM] + [VMEM] * 6,
            [
                pltpu.VMEM((RING, tokens, narrow), jnp.bfloat16),
                pltpu.VMEM((RING, tokens, hidden + 128), jnp.bfloat16),
            ],
            flops=product,
            nbytes=2 * narrow * hidden,
        )(place, *gather_behind(x, "y"), up_own, up_other)
        act = call(
            lambda *refs: act_kernel(width, *refs), acted, [VMEM] * RING, nbytes=8 * tokens * hidden
        )(*send_each(parts, "z"))
        parts = call(
            down_kernel,
            [block] * RING,
            [SMEM] + [VMEM] * 6,
            [
                pltpu.VMEM((RING, tokens, hidden), jnp.bfloat16),
                pltpu.VMEM((RING, tokens, narrow), jnp.bfloat16),
            ],
            flops=product,
            nbytes=2 * narrow * hidden,
        )(place, *gather_behind(act, "z"), down_own, down_other)
        total = sum(t.astype(jnp.float32) for t in send_each(parts, "y"))
        x = (x.astype(jnp.float32) + total).astype(jnp.bfloat16)

    quarters = x.reshape(tokens, 2, 2, half)
    quarters = jnp.where(first, quarters, quarters[:, :, ::-1])
    low, high = (quarters[:, i].reshape(tokens, 2 * half) for i in range(2))
    even = z % 2 == 0
    one = grid_move(
        jnp.where(even, low, high), lambda a, b: (b // 2 if b % 2 == 0 else 2 + b // 2, a)
    )
    two = grid_move(
        jnp.where(even, high, low), lambda a, b: (2 + b // 2 if b % 2 == 0 else b // 2, a)
    )
    front = y < 2
    out = jnp.concatenate([jnp.where(front, one, two), jnp.where(front, two, one)], axis=1)
    return out[None]


def solution(mesh):
    inner = Mesh(mesh.devices.reshape(SIZES), AXES)
    section, field, dp = ("xh", "core"), "y", ("xl", "z")
    in_specs = (
        P(None, dp, field, None),
        P(None, dp, field),
        P(),
        P(field, None, None),
        P(field, None),
        P(section, None),
        P(section, dp, field),
        P(section, field, dp),
    )
    return jax.shard_map(
        per_device, mesh=inner, in_specs=in_specs, out_specs=P(section, dp, field), check_vma=False
    )
```

```python
import jax
import jax.numpy as jnp
from jax import lax
from jax.experimental import pallas as pl
from jax.experimental.pallas import tpu as pltpu
from jax.sharding import Mesh, PartitionSpec as P

AXES = ("xh", "core", "y", "xl", "z")
SIZES = (2, 2, 4, 2, 4)
RING = 4
EPS = 1e-05
SMEM = pl.BlockSpec(memory_space=pltpu.SMEM)
ANY = pl.BlockSpec(memory_space=pl.ANY)


def call(kernel, out_shape, operands, specs, scratch=(), after=()):
    kept = len(operands)

    def body(*refs):
        kernel(*refs[:kept], *refs[kept + len(after) :])

    return pl.pallas_call(
        body,
        grid=(1,),
        out_shape=out_shape,
        in_specs=list(specs) + [whole(v) for v in after],
        out_specs=jax.tree.map(whole, out_shape),
        scratch_shapes=list(scratch),
        compiler_params=pltpu.CompilerParams(vmem_limit_bytes=24 * 2**20),
        cost_estimate=pl.CostEstimate(flops=0, bytes_accessed=0, transcendentals=0),
    )(*operands, *after)


def whole(like):
    return pl.BlockSpec(like.shape, lambda _: (0,) * len(like.shape))


def pair_of(like, pair):
    return pl.BlockSpec((2,) + like.shape[1:], lambda _: (pair,) + (0,) * (len(like.shape) - 1))


def pass_on(array, after):
    def body(*refs):
        pass

    return pl.pallas_call(
        body,
        out_shape=jax.ShapeDtypeStruct(array.shape, array.dtype),
        grid=(1,),
        in_specs=[ANY, whole(after)],
        out_specs=ANY,
        input_output_aliases={0: 0},
    )(array, after)


def embed_kernel(place, m0, m1, m2, m3, bias, table, *rest):
    outs, token, held, made = rest[:RING], *rest[RING:]
    token[...] = jnp.zeros(token.shape, token.dtype)
    y, z = place[1], place[2]
    depth, half = table.shape[1:]
    for behind, block in enumerate((m0, m1, m2, m3)):
        held[lax.rem(z + RING - behind, RING)] = block[...]
    rows = RING * m0.shape[0]
    pieces = held[...].reshape(rows, held.shape[2])
    present = pieces[:, depth : depth + 128].astype(jnp.float32)
    for k in range(4):
        total = jnp.dot(pieces[:, :depth], table[k], preferred_element_type=jnp.float32)
        for f in range(2):
            total += present[:, f : f + 1] * bias[k, f : f + 1].astype(jnp.float32)
        total = total.astype(jnp.bfloat16).reshape(RING, rows // RING, half)
        made[:, :, k * half : (k + 1) * half] = total
    for ahead in range(RING):
        outs[ahead][...] = made[lax.rem(y + ahead, RING)]


def up_kernel(place, first, second, own, other, *rest):
    outs, token, made = rest[:RING], *rest[RING:]
    token[...] = jnp.zeros(token.shape, token.dtype)
    z = place[2]
    tokens, hidden, half = first.shape[0], own.shape[2], own.shape[1]
    rows, small = 2 * tokens, tokens // RING
    x = jnp.concatenate([first[...], second[...]], axis=0)
    for start in range(0, hidden, 256):
        wide = min(256, hidden - start)
        at = slice(start, start + wide)
        total = jnp.zeros((rows, wide), jnp.float32)
        for xl in range(2):
            for rel, part in enumerate((own, other)):
                k = (xl * 2 + rel) * half
                total += jnp.dot(
                    x[:, k : k + half], part[xl, :, at], preferred_element_type=jnp.float32
                )
        made[:, :, at] = total.astype(jnp.bfloat16).reshape(2 * RING, small, wide)
    values = x.astype(jnp.float32)
    square = jnp.sum(values * values, axis=1, keepdims=True)
    high = square.astype(jnp.bfloat16).astype(jnp.float32)
    lane = lax.broadcasted_iota(jnp.int32, (rows, 128), 1)
    tail = jnp.where(lane == 0, high, jnp.where(lane == 1, square - high, 0.0))
    made[:, :, hidden:] = tail.astype(jnp.bfloat16).reshape(2 * RING, small, 128)
    for ahead in range(RING):
        part = lax.rem(z + ahead, RING)
        outs[ahead][:small] = made[part]
        outs[ahead][small:] = made[RING + part]


def act_kernel(width, h0, h1, h2, h3, out, token):
    token[...] = jnp.zeros(token.shape, token.dtype)
    hidden = out.shape[1]
    blocks = (h0, h1, h2, h3)
    square = jnp.zeros((out.shape[0], 1), jnp.float32)
    for block in blocks:
        tail = block[:, hidden:].astype(jnp.float32)
        square += jnp.sum(tail, axis=1, keepdims=True)
    scale = lax.rsqrt(square / width + EPS)
    total = jnp.zeros(out.shape, jnp.float32)
    for block in blocks:
        total += block[:, :hidden].astype(jnp.float32)
    out[...] = jax.nn.gelu(total * scale, approximate=True).astype(jnp.bfloat16)


def down_kernel(place, a0, a1, a2, a3, own, other, *rest):
    outs, token, held = rest[:2], *rest[2:]
    token[...] = jnp.zeros(token.shape, token.dtype)
    z = place[2]
    small, half = a0.shape[0] // 2, own.shape[2]
    for behind, block in enumerate((a0, a1, a2, a3)):
        part = lax.rem(z + RING - behind, RING)
        held[part] = block[:small]
        held[RING + part] = block[small:]
    tokens = RING * small
    act = held[...].reshape(2 * tokens, held.shape[2])
    for xl in range(2):
        for rel, part in enumerate((own, other)):
            k = (xl * 2 + rel) * half
            total = jnp.dot(act, part[xl], preferred_element_type=jnp.float32)
            total = total.astype(jnp.bfloat16)
            outs[0][:, k : k + half] = total[:tokens]
            outs[1][:, k : k + half] = total[tokens:]


def add_kernel(*refs):
    *terms, out, token = refs
    token[...] = jnp.zeros(token.shape, token.dtype)
    out[...] = sum(t[...].astype(jnp.float32) for t in terms).astype(out.dtype)


def last_kernel(place, part, first, second, one, two):
    total = sum(t[...].astype(jnp.float32) for t in (part, first, second)).astype(jnp.bfloat16)
    half = total.shape[1] // 4
    odd = lax.rem(place[2], 2)
    for xl in range(2):
        for rel in range(2):
            k = (xl * 2 + rel) * half
            piece = total[:, k : k + half]
            side = place[0] if rel == 0 else 1 - place[0]
            at = pl.ds(pl.multiple_of(side * half, half), half)

            @pl.when(odd == xl)
            def _():
                one[:, at] = piece

            @pl.when(odd != xl)
            def _():
                two[:, at] = piece


def to_ahead(block, axis, distance):
    return lax.ppermute(block, axis, [(i, (i + distance) % RING) for i in range(RING)])


def send_each(blocks, axis):
    moved = {d: to_ahead(blocks[d], axis, d) for d in (2, 1, 3)}
    return [blocks[0], moved[1], moved[2], moved[3]]


def gather_behind(block, axis):
    return send_each([block] * RING, axis)


def gather_x(block):
    return lax.all_gather(block, ("xh", "xl"), axis=0, tiled=False)


def swap_core(block):
    return lax.ppermute(block, "core", [(0, 1), (1, 0)])


def grid_move(block, target):
    route = [
        (y * RING + z, target(y, z)[0] * RING + target(y, z)[1])
        for y in range(RING)
        for z in range(RING)
    ]
    return lax.ppermute(block, ("y", "z"), route)


def per_device(patches, field_mask, order, embed_weight, embed_bias, norm_gain, w_up, w_down):
    xh, core, y, xl, z = (lax.axis_index(name) for name in AXES)
    first = core == 0
    tokens = patches.shape[1]
    width = embed_weight.shape[2]
    rows_up = w_up.shape[1]
    hidden = w_up.shape[2]
    half = rows_up // 2
    narrow = width // RING
    place = jnp.stack([core, y, z, 2 * xh + core]).astype(jnp.int32)

    gain = lax.dynamic_slice(norm_gain[0], ((xl * RING + z) * rows_up,), (rows_up,))
    up = (w_up[0].astype(jnp.float32) * gain[:, None]).astype(jnp.bfloat16)
    down = w_down[0]
    up_low, up_high = up[:half], up[half:]
    up_got = swap_core(jnp.where(first, up_high, up_low))
    ups = [gather_x(jnp.where(first, up_low, up_got)), jnp.where(first, up_got, up_high)]

    flat = lax.optimization_barrier(patches.reshape(patches.shape[0], tokens, -1))
    chosen = order[place[3]]
    piece = lax.dynamic_index_in_dim(flat, chosen, 0, keepdims=False)
    present = lax.dynamic_index_in_dim(field_mask, chosen, 0, keepdims=False)
    present = present.astype(jnp.bfloat16)
    depth = patches.shape[3]
    masked = [piece[:, f * depth : (f + 1) * depth] * present[:, f : f + 1] for f in range(2)]
    message = jnp.concatenate([*masked, jnp.pad(present, ((0, 0), (0, 126)))], axis=1)
    later = message[0, 0].astype(jnp.float32) * 0.0
    first_later = core.astype(jnp.float32) + later == 0.0
    down_low, down_high = down[:, :half], down[:, half:]
    down_got = swap_core(jnp.where(first_later, down_high, down_low))
    downs = [gather_x(jnp.where(first, down_low, down_got))]
    ups[1] = gather_x(ups[1])
    downs.append(gather_x(jnp.where(first, down_got, down_high)))

    table = embed_weight.reshape(-1, width)
    block = jax.ShapeDtypeStruct((tokens, narrow), jnp.bfloat16)
    partial = jax.ShapeDtypeStruct((tokens, narrow), jnp.float32)
    token = jax.ShapeDtypeStruct((8, 128), jnp.float32)
    starts = [
        (z + RING * xl) * (2 * half) + (core if rel == 0 else 1 - core) * half
        for xl in range(2)
        for rel in range(2)
    ]
    table, bias = (
        jnp.stack([lax.dynamic_slice_in_dim(v, at, half, 1) for at in starts])
        for v in (table, embed_bias)
    )
    operands = [*gather_behind(message, "z"), bias, table]
    *terms, seen = call(
        embed_kernel,
        [block] * RING + [token],
        [place, *operands],
        [SMEM] + [whole(v) for v in operands],
        [
            pltpu.VMEM((RING,) + message.shape, jnp.bfloat16),
            pltpu.VMEM((RING, tokens, narrow), jnp.bfloat16),
        ],
    )
    terms = send_each(terms, "y")

    def add_of(terms, like):
        specs = [whole(t) for t in terms]
        return call(add_kernel, [like, token], terms, specs)

    x, seen_some = add_of((terms[0], terms[2]), partial)
    x, seen_x = add_of((x, terms[1], terms[3]), block)

    small = tokens // RING
    sent = jax.ShapeDtypeStruct((2 * small, hidden + 128), jnp.bfloat16)
    acted = jax.ShapeDtypeStruct((2 * small, hidden), jnp.bfloat16)

    def up_of(blocks, weights, pair, after=()):
        return call(
            up_kernel,
            [sent] * RING + [token],
            [place, *blocks, *weights],
            [SMEM] + [whole(block)] * 2 + [pair_of(w, pair) for w in weights],
            [pltpu.VMEM((2 * RING, small, hidden + 128), jnp.bfloat16)],
            after,
        )

    def act_of(parts, after=()):
        return call(
            lambda *refs: act_kernel(width, *refs),
            [acted, token],
            parts,
            [whole(sent)] * RING,
            (),
            after,
        )

    def down_of(acts, weights, pair, after=()):
        return call(
            down_kernel,
            [block] * 2 + [token],
            [place, *acts, *weights],
            [SMEM] + [whole(acted)] * RING + [pair_of(w, pair) for w in weights],
            [pltpu.VMEM((2 * RING, small, hidden), jnp.bfloat16)],
            after,
        )

    ready = {}
    for layer in range(4):
        kind, pair = layer % 2, layer // 2
        if pair == 0:
            held = pass_on(ups[kind], seen_some if kind == 0 else seen_x)
            ready["up", kind] = (held, swap_core(held))
        x0, x1, x2, x3 = gather_behind(x, "y")
        *parts, up_a = up_of((x0, x2), ready["up", kind], pair)
        h_a = send_each(parts, "z")
        *parts, up_b = up_of((x1, x3), ready["up", kind], pair, (up_a,))
        h_b = send_each(parts, "z")
        act, seen_a = act_of(h_a, (up_b,))
        acts_a = gather_behind(act, "z")
        act, seen_b = act_of(h_b, (seen_a,))
        acts_b = gather_behind(act, "z")
        if pair == 0:
            held = pass_on(downs[kind], seen_a if kind == 0 else seen_b)
            ready["down", kind] = (held, swap_core(held))
        mine, second, down_a = down_of(acts_a, ready["down", kind], pair, (seen_b,))
        second = to_ahead(second, "y", 2)
        first_back, third_back, _ = down_of(acts_b, ready["down", kind], pair, (down_a,))
        first_back = to_ahead(first_back, "y", 3)
        third_back = to_ahead(third_back, "y", 1)
        x, _ = add_of((x, mine, second), partial)
        if layer < 3:
            x, seen_x = add_of((x, first_back, third_back), block)

    out = jax.ShapeDtypeStruct((tokens, 2 * half), jnp.bfloat16)
    last = [x, first_back, third_back]
    one, two = call(last_kernel, [out, out], [place, *last], [SMEM] + [whole(v) for v in last])
    one = grid_move(
        one, lambda a, b: (b // 2 if b % 2 == 0 else 2 + b // 2, a)
    )
    two = grid_move(
        two, lambda a, b: (2 + b // 2 if b % 2 == 0 else b // 2, a)
    )
    front = y < 2
    out = jnp.concatenate([jnp.where(front, one, two), jnp.where(front, two, one)], axis=1)
    return out[None]


def solution(mesh):
    inner = Mesh(mesh.devices.reshape(SIZES), AXES)
    section, field, dp = ("xh", "core"), "y", ("xl", "z")
    in_specs = (
        P(None, dp, field, None),
        P(None, dp, field),
        P(),
        P(field, None, None),
        P(field, None),
        P(section, None),
        P(section, dp, field),
        P(section, field, dp),
    )
    return jax.shard_map(
        per_device, mesh=inner, in_specs=in_specs, out_specs=P(section, dp, field), check_vma=False
    )
```

```python
import jax
import jax.numpy as jnp
from jax import lax
from jax.experimental import pallas as pl
from jax.experimental.pallas import tpu as pltpu
from jax.sharding import Mesh, PartitionSpec as P

AXES = ("xh", "core", "y", "xl", "z")
SIZES = (2, 2, 4, 2, 4)
RING = 4
EPS = 1e-05
SMEM = pl.BlockSpec(memory_space=pltpu.SMEM)
ANY = pl.BlockSpec(memory_space=pl.ANY)


def call(kernel, out_shape, operands, specs, scratch=(), after=()):
    kept = len(operands)

    def body(*refs):
        kernel(*refs[:kept], *refs[kept + len(after) :])

    return pl.pallas_call(
        body,
        grid=(1,),
        out_shape=out_shape,
        in_specs=list(specs) + [whole(v) for v in after],
        out_specs=jax.tree.map(whole, out_shape),
        scratch_shapes=list(scratch),
        compiler_params=pltpu.CompilerParams(vmem_limit_bytes=16 * 2**20),
        cost_estimate=pl.CostEstimate(flops=0, bytes_accessed=0, transcendentals=0),
    )(*operands, *after)


def whole(like):
    return pl.BlockSpec(like.shape, lambda _: (0,) * len(like.shape))


def pair_of(like, pair):
    return pl.BlockSpec((2,) + like.shape[1:], lambda _: (pair,) + (0,) * (len(like.shape) - 1))


def pass_on(array, after):
    def body(*refs):
        pass

    return pl.pallas_call(
        body,
        out_shape=jax.ShapeDtypeStruct(array.shape, array.dtype),
        grid=(1,),
        in_specs=[ANY, whole(after)],
        out_specs=ANY,
        input_output_aliases={0: 0},
    )(array, after)


def embed_kernel(place, m0, m1, m2, m3, bias, table, *rest):
    outs, token, held, made = rest[:RING], *rest[RING:]
    token[...] = jnp.zeros(token.shape, token.dtype)
    y, z = place[1], place[2]
    depth, half = table.shape[1:]
    for behind, block in enumerate((m0, m1, m2, m3)):
        held[lax.rem(z + RING - behind, RING)] = block[...]
    rows = RING * m0.shape[0]
    pieces = held[...].reshape(rows, held.shape[2])
    present = pieces[:, depth : depth + 128].astype(jnp.float32)
    for k in range(4):
        total = jnp.dot(pieces[:, :depth], table[k], preferred_element_type=jnp.float32)
        for f in range(2):
            total += present[:, f : f + 1] * bias[k, f : f + 1].astype(jnp.float32)
        total = total.astype(jnp.bfloat16).reshape(RING, rows // RING, half)
        made[:, :, k * half : (k + 1) * half] = total
    for ahead in range(RING):
        outs[ahead][...] = made[lax.rem(y + ahead, RING)]


def up_kernel(place, first, second, own, other, *rest):
    outs, token, made = rest[:RING], *rest[RING:]
    token[...] = jnp.zeros(token.shape, token.dtype)
    z = place[2]
    tokens, hidden, half = first.shape[0], own.shape[2], own.shape[1]
    rows, small = 2 * tokens, tokens // RING
    x = jnp.concatenate([first[...], second[...]], axis=0)
    for start in range(0, hidden, 256):
        wide = min(256, hidden - start)
        at = slice(start, start + wide)
        total = jnp.zeros((rows, wide), jnp.float32)
        for xl in range(2):
            for rel, part in enumerate((own, other)):
                k = (xl * 2 + rel) * half
                total += jnp.dot(
                    x[:, k : k + half], part[xl, :, at], preferred_element_type=jnp.float32
                )
        made[:, :, at] = total.astype(jnp.bfloat16).reshape(2 * RING, small, wide)
    values = x.astype(jnp.float32)
    square = jnp.sum(values * values, axis=1, keepdims=True)
    high = square.astype(jnp.bfloat16).astype(jnp.float32)
    lane = lax.broadcasted_iota(jnp.int32, (rows, 128), 1)
    tail = jnp.where(lane == 0, high, jnp.where(lane == 1, square - high, 0.0))
    made[:, :, hidden:] = tail.astype(jnp.bfloat16).reshape(2 * RING, small, 128)
    for ahead in range(RING):
        part = lax.rem(z + ahead, RING)
        outs[ahead][:small] = made[part]
        outs[ahead][small:] = made[RING + part]


def act_kernel(width, h0, h1, h2, h3, out, token):
    token[...] = jnp.zeros(token.shape, token.dtype)
    hidden = out.shape[1]
    blocks = (h0, h1, h2, h3)
    square = jnp.zeros((out.shape[0], 1), jnp.float32)
    for block in blocks:
        tail = block[:, hidden:].astype(jnp.float32)
        square += jnp.sum(tail, axis=1, keepdims=True)
    scale = lax.rsqrt(square / width + EPS)
    total = jnp.zeros(out.shape, jnp.float32)
    for block in blocks:
        total += block[:, :hidden].astype(jnp.float32)
    out[...] = jax.nn.gelu(total * scale, approximate=True).astype(jnp.bfloat16)


def down_kernel(place, a0, a1, a2, a3, own, other, *rest):
    outs, token, held = rest[:2], *rest[2:]
    token[...] = jnp.zeros(token.shape, token.dtype)
    z = place[2]
    small, half = a0.shape[0] // 2, own.shape[2]
    for behind, block in enumerate((a0, a1, a2, a3)):
        part = lax.rem(z + RING - behind, RING)
        held[part] = block[:small]
        held[RING + part] = block[small:]
    tokens = RING * small
    act = held[...].reshape(2 * tokens, held.shape[2])
    for xl in range(2):
        for rel, part in enumerate((own, other)):
            k = (xl * 2 + rel) * half
            total = jnp.dot(act, part[xl], preferred_element_type=jnp.float32)
            total = total.astype(jnp.bfloat16)
            outs[0][:, k : k + half] = total[:tokens]
            outs[1][:, k : k + half] = total[tokens:]


def add_kernel(*refs):
    *terms, out, token = refs
    token[...] = jnp.zeros(token.shape, token.dtype)
    out[...] = sum(t[...].astype(jnp.float32) for t in terms).astype(out.dtype)


def last_kernel(place, part, first, second, one, two):
    total = sum(t[...].astype(jnp.float32) for t in (part, first, second)).astype(jnp.bfloat16)
    half = total.shape[1] // 4
    odd = lax.rem(place[2], 2)
    for xl in range(2):
        for rel in range(2):
            k = (xl * 2 + rel) * half
            piece = total[:, k : k + half]
            side = place[0] if rel == 0 else 1 - place[0]
            at = pl.ds(pl.multiple_of(side * half, half), half)

            @pl.when(odd == xl)
            def _():
                one[:, at] = piece

            @pl.when(odd != xl)
            def _():
                two[:, at] = piece


def to_ahead(block, axis, distance):
    return lax.ppermute(block, axis, [(i, (i + distance) % RING) for i in range(RING)])


def send_each(blocks, axis):
    moved = {d: to_ahead(blocks[d], axis, d) for d in (2, 1, 3)}
    return [blocks[0], moved[1], moved[2], moved[3]]


def gather_behind(block, axis):
    return send_each([block] * RING, axis)


def gather_x(block):
    return lax.all_gather(block, ("xh", "xl"), axis=0, tiled=False)


def swap_core(block):
    return lax.ppermute(block, "core", [(0, 1), (1, 0)])


def grid_move(block, target):
    route = [
        (y * RING + z, target(y, z)[0] * RING + target(y, z)[1])
        for y in range(RING)
        for z in range(RING)
    ]
    return lax.ppermute(block, ("y", "z"), route)


def per_device(patches, field_mask, order, embed_weight, embed_bias, norm_gain, w_up, w_down):
    xh, core, y, xl, z = (lax.axis_index(name) for name in AXES)
    first = core == 0
    tokens = patches.shape[1]
    width = embed_weight.shape[2]
    rows_up = w_up.shape[1]
    hidden = w_up.shape[2]
    half = rows_up // 2
    narrow = width // RING
    place = jnp.stack([core, y, z, 2 * xh + core]).astype(jnp.int32)

    gain = lax.dynamic_slice(norm_gain[0], ((xl * RING + z) * rows_up,), (rows_up,))
    up = (w_up[0].astype(jnp.float32) * gain[:, None]).astype(jnp.bfloat16)
    down = w_down[0]
    up_low, up_high = up[:half], up[half:]
    up_got = swap_core(jnp.where(first, up_high, up_low))
    ups = [gather_x(jnp.where(first, up_low, up_got)), jnp.where(first, up_got, up_high)]

    down_low, down_high = down[:, :half], down[:, half:]
    down_got = swap_core(jnp.where(first, down_high, down_low))
    downs = [gather_x(jnp.where(first, down_low, down_got))]
    ups[1] = gather_x(ups[1])
    downs.append(gather_x(jnp.where(first, down_got, down_high)))

    flat = lax.optimization_barrier(patches.reshape(patches.shape[0], tokens, -1))
    chosen = order[place[3]]
    piece = lax.dynamic_index_in_dim(flat, chosen, 0, keepdims=False)
    present = lax.dynamic_index_in_dim(field_mask, chosen, 0, keepdims=False)
    present = present.astype(jnp.bfloat16)
    depth = patches.shape[3]
    masked = [piece[:, f * depth : (f + 1) * depth] * present[:, f : f + 1] for f in range(2)]
    message = jnp.concatenate([*masked, jnp.pad(present, ((0, 0), (0, 126)))], axis=1)
    table = embed_weight.reshape(-1, width)
    block = jax.ShapeDtypeStruct((tokens, narrow), jnp.bfloat16)
    partial = jax.ShapeDtypeStruct((tokens, narrow), jnp.float32)
    token = jax.ShapeDtypeStruct((8, 128), jnp.float32)
    starts = [
        (z + RING * xl) * (2 * half) + (core if rel == 0 else 1 - core) * half
        for xl in range(2)
        for rel in range(2)
    ]
    table, bias = (
        jnp.stack([lax.dynamic_slice_in_dim(v, at, half, 1) for at in starts])
        for v in (table, embed_bias)
    )
    operands = [*gather_behind(message, "z"), bias, table]
    *terms, seen = call(
        embed_kernel,
        [block] * RING + [token],
        [place, *operands],
        [SMEM] + [whole(v) for v in operands],
        [
            pltpu.VMEM((RING,) + message.shape, jnp.bfloat16),
            pltpu.VMEM((RING, tokens, narrow), jnp.bfloat16),
        ],
    )
    terms = send_each(terms, "y")

    def add_of(terms, like):
        specs = [whole(t) for t in terms]
        return call(add_kernel, [like, token], terms, specs)

    x, _ = add_of((terms[0], terms[2]), partial)
    x, seen_x = add_of((x, terms[1], terms[3]), block)

    small = tokens // RING
    sent = jax.ShapeDtypeStruct((2 * small, hidden + 128), jnp.bfloat16)
    acted = jax.ShapeDtypeStruct((2 * small, hidden), jnp.bfloat16)

    def up_of(blocks, weights, pair, after=()):
        return call(
            up_kernel,
            [sent] * RING + [token],
            [place, *blocks, *weights],
            [SMEM] + [whole(block)] * 2 + [pair_of(w, pair) for w in weights],
            [pltpu.VMEM((2 * RING, small, hidden + 128), jnp.bfloat16)],
            after,
        )

    def act_of(parts, after=()):
        return call(
            lambda *refs: act_kernel(width, *refs),
            [acted, token],
            parts,
            [whole(sent)] * RING,
            (),
            after,
        )

    def down_of(acts, weights, pair, after=()):
        return call(
            down_kernel,
            [block] * 2 + [token],
            [place, *acts, *weights],
            [SMEM] + [whole(acted)] * RING + [pair_of(w, pair) for w in weights],
            [pltpu.VMEM((2 * RING, small, hidden), jnp.bfloat16)],
            after,
        )

    ready = {}
    for layer in range(4):
        kind, pair = layer % 2, layer // 2
        if pair == 0:
            held = pass_on(ups[kind], seen_x)
            ready["up", kind] = (held, swap_core(held))
        x0, x1, x2, x3 = gather_behind(x, "y")
        *parts, up_a = up_of((x0, x2), ready["up", kind], pair)
        h_a = send_each(parts, "z")
        *parts, up_b = up_of((x1, x3), ready["up", kind], pair, (up_a,))
        h_b = send_each(parts, "z")
        act, seen_a = act_of(h_a, (up_b,))
        acts_a = gather_behind(act, "z")
        act, seen_b = act_of(h_b, (seen_a, acts_a[2]) if pair == 0 else (seen_a,))
        acts_b = gather_behind(act, "z")
        if pair == 0:
            held = pass_on(downs[kind], seen_b)
            ready["down", kind] = (held, swap_core(held))
        mine, second, down_a = down_of(acts_a, ready["down", kind], pair, (seen_b,))
        second = to_ahead(second, "y", 2)
        first_back, third_back, _ = down_of(acts_b, ready["down", kind], pair, (down_a,))
        first_back = to_ahead(first_back, "y", 3)
        third_back = to_ahead(third_back, "y", 1)
        x, _ = add_of((x, mine, second), partial)
        if layer < 3:
            x, seen_x = add_of((x, first_back, third_back), block)

    out = jax.ShapeDtypeStruct((tokens, 2 * half), jnp.bfloat16)
    last = [x, first_back, third_back]
    one, two = call(last_kernel, [out, out], [place, *last], [SMEM] + [whole(v) for v in last])
    one = grid_move(
        one, lambda a, b: (b // 2 if b % 2 == 0 else 2 + b // 2, a)
    )
    two = grid_move(
        two, lambda a, b: (2 + b // 2 if b % 2 == 0 else b // 2, a)
    )
    front = y < 2
    out = jnp.concatenate([jnp.where(front, one, two), jnp.where(front, two, one)], axis=1)
    return out[None]


def solution(mesh):
    inner = Mesh(mesh.devices.reshape(SIZES), AXES)
    section, field, dp = ("xh", "core"), "y", ("xl", "z")
    in_specs = (
        P(None, dp, field, None),
        P(None, dp, field),
        P(),
        P(field, None, None),
        P(field, None),
        P(section, None),
        P(section, dp, field),
        P(section, field, dp),
    )
    return jax.shard_map(
        per_device, mesh=inner, in_specs=in_specs, out_specs=P(section, dp, field), check_vma=False
    )
```

```python
import jax
import jax.numpy as jnp
from jax import lax
from jax.experimental import pallas as pl
from jax.experimental.pallas import tpu as pltpu
from jax.sharding import Mesh, PartitionSpec as P

AXES = ("xh", "core", "y", "xl", "z")
SIZES = (2, 2, 4, 2, 4)
RING = 4
EPS = 1e-05
SMEM = pl.BlockSpec(memory_space=pltpu.SMEM)
ANY = pl.BlockSpec(memory_space=pl.ANY)


def call(kernel, out_shape, operands, specs, scratch=(), after=()):
    kept = len(operands)

    def body(*refs):
        kernel(*refs[:kept], *refs[kept + len(after) :])

    return pl.pallas_call(
        body,
        grid=(1,),
        out_shape=out_shape,
        in_specs=list(specs) + [whole(v) for v in after],
        out_specs=jax.tree.map(whole, out_shape),
        scratch_shapes=list(scratch),
        compiler_params=pltpu.CompilerParams(vmem_limit_bytes=16 * 2**20),
        cost_estimate=pl.CostEstimate(flops=0, bytes_accessed=0, transcendentals=0),
    )(*operands, *after)


def whole(like):
    return pl.BlockSpec(like.shape, lambda _: (0,) * len(like.shape))


def pair_of(like, pair):
    return pl.BlockSpec((2,) + like.shape[1:], lambda _: (pair,) + (0,) * (len(like.shape) - 1))


def pass_on(array, after):
    def body(*refs):
        pass

    return pl.pallas_call(
        body,
        out_shape=jax.ShapeDtypeStruct(array.shape, array.dtype),
        grid=(1,),
        in_specs=[ANY, whole(after)],
        out_specs=ANY,
        input_output_aliases={0: 0},
    )(array, after)


def embed_kernel(place, m0, m1, m2, m3, bias, table, *rest):
    outs, token, held, made = rest[:RING], *rest[RING:]
    token[...] = jnp.zeros(token.shape, token.dtype)
    y, z = place[1], place[2]
    depth, half = table.shape[1:]
    for behind, block in enumerate((m0, m1, m2, m3)):
        held[lax.rem(z + RING - behind, RING)] = block[...]
    rows = RING * m0.shape[0]
    pieces = held[...].reshape(rows, held.shape[2])
    present = pieces[:, depth : depth + 128].astype(jnp.float32)
    for k in range(4):
        total = jnp.dot(pieces[:, :depth], table[k], preferred_element_type=jnp.float32)
        for f in range(2):
            total += present[:, f : f + 1] * bias[k, f : f + 1].astype(jnp.float32)
        total = total.astype(jnp.bfloat16).reshape(RING, rows // RING, half)
        made[:, :, k * half : (k + 1) * half] = total
    for ahead in range(RING):
        outs[ahead][...] = made[lax.rem(y + ahead, RING)]


def up_kernel(place, first, second, own, other, *rest):
    outs, token, made = rest[:RING], *rest[RING:]
    token[...] = jnp.zeros(token.shape, token.dtype)
    z = place[2]
    tokens, hidden, half = first.shape[0], own.shape[2], own.shape[1]
    rows, small = 2 * tokens, tokens // RING
    x = jnp.concatenate([first[...], second[...]], axis=0)
    for start in range(0, hidden, 256):
        wide = min(256, hidden - start)
        at = slice(start, start + wide)
        total = jnp.zeros((rows, wide), jnp.float32)
        for xl in range(2):
            for rel, part in enumerate((own, other)):
                k = (xl * 2 + rel) * half
                total += jnp.dot(
                    x[:, k : k + half], part[xl, :, at], preferred_element_type=jnp.float32
                )
        made[:, :, at] = total.astype(jnp.bfloat16).reshape(2 * RING, small, wide)
    values = x.astype(jnp.float32)
    square = jnp.sum(values * values, axis=1, keepdims=True)
    high = square.astype(jnp.bfloat16).astype(jnp.float32)
    lane = lax.broadcasted_iota(jnp.int32, (rows, 128), 1)
    tail = jnp.where(lane == 0, high, jnp.where(lane == 1, square - high, 0.0))
    made[:, :, hidden:] = tail.astype(jnp.bfloat16).reshape(2 * RING, small, 128)
    for ahead in range(RING):
        part = lax.rem(z + ahead, RING)
        outs[ahead][:small] = made[part]
        outs[ahead][small:] = made[RING + part]


def act_kernel(width, h0, h1, h2, h3, out, token):
    token[...] = jnp.zeros(token.shape, token.dtype)
    hidden = out.shape[1]
    blocks = (h0, h1, h2, h3)
    square = jnp.zeros((out.shape[0], 1), jnp.float32)
    for block in blocks:
        tail = block[:, hidden:].astype(jnp.float32)
        square += jnp.sum(tail, axis=1, keepdims=True)
    scale = lax.rsqrt(square / width + EPS)
    total = jnp.zeros(out.shape, jnp.float32)
    for block in blocks:
        total += block[:, :hidden].astype(jnp.float32)
    out[...] = jax.nn.gelu(total * scale, approximate=True).astype(jnp.bfloat16)


def down_kernel(place, a0, a1, a2, a3, own, other, *rest):
    outs, token, held = rest[:2], *rest[2:]
    token[...] = jnp.zeros(token.shape, token.dtype)
    z = place[2]
    small, half = a0.shape[0] // 2, own.shape[2]
    for behind, block in enumerate((a0, a1, a2, a3)):
        part = lax.rem(z + RING - behind, RING)
        held[part] = block[:small]
        held[RING + part] = block[small:]
    tokens = RING * small
    act = held[...].reshape(2 * tokens, held.shape[2])
    for xl in range(2):
        for rel, part in enumerate((own, other)):
            k = (xl * 2 + rel) * half
            total = jnp.dot(act, part[xl], preferred_element_type=jnp.float32)
            total = total.astype(jnp.bfloat16)
            outs[0][:, k : k + half] = total[:tokens]
            outs[1][:, k : k + half] = total[tokens:]


def add_kernel(*refs):
    *terms, out, token = refs
    token[...] = jnp.zeros(token.shape, token.dtype)
    out[...] = sum(t[...].astype(jnp.float32) for t in terms).astype(out.dtype)


def last_kernel(place, part, first, second, one, two):
    total = sum(t[...].astype(jnp.float32) for t in (part, first, second)).astype(jnp.bfloat16)
    half = total.shape[1] // 4
    odd = lax.rem(place[2], 2)
    for xl in range(2):
        for rel in range(2):
            k = (xl * 2 + rel) * half
            piece = total[:, k : k + half]
            side = place[0] if rel == 0 else 1 - place[0]
            at = pl.ds(pl.multiple_of(side * half, half), half)

            @pl.when(odd == xl)
            def _():
                one[:, at] = piece

            @pl.when(odd != xl)
            def _():
                two[:, at] = piece


def to_ahead(block, axis, distance):
    return lax.ppermute(block, axis, [(i, (i + distance) % RING) for i in range(RING)])


def send_each(blocks, axis):
    moved = {d: to_ahead(blocks[d], axis, d) for d in (2, 1, 3)}
    return [blocks[0], moved[1], moved[2], moved[3]]


def gather_behind(block, axis):
    return send_each([block] * RING, axis)


def gather_x(block):
    return lax.all_gather(block, ("xh", "xl"), axis=0, tiled=False)


def swap_core(block):
    return lax.ppermute(block, "core", [(0, 1), (1, 0)])


def grid_move(block, target):
    route = [
        (y * RING + z, target(y, z)[0] * RING + target(y, z)[1])
        for y in range(RING)
        for z in range(RING)
    ]
    return lax.ppermute(block, ("y", "z"), route)


def per_device(patches, field_mask, order, embed_weight, embed_bias, norm_gain, w_up, w_down):
    xh, core, y, xl, z = (lax.axis_index(name) for name in AXES)
    first = core == 0
    tokens = patches.shape[1]
    width = embed_weight.shape[2]
    rows_up = w_up.shape[1]
    hidden = w_up.shape[2]
    half = rows_up // 2
    narrow = width // RING
    place = jnp.stack([core, y, z, 2 * xh + core]).astype(jnp.int32)

    gain = lax.dynamic_slice(norm_gain[0], ((xl * RING + z) * rows_up,), (rows_up,))
    up = (w_up[0].astype(jnp.float32) * gain[:, None]).astype(jnp.bfloat16)
    down = w_down[0]
    up_low, up_high = up[:half], up[half:]
    up_got = swap_core(jnp.where(first, up_high, up_low))
    ups = [gather_x(jnp.where(first, up_low, up_got)), jnp.where(first, up_got, up_high)]

    down_low, down_high = down[:, :half], down[:, half:]
    down_got = swap_core(jnp.where(first, down_high, down_low))
    downs = [gather_x(jnp.where(first, down_low, down_got))]
    ups[1] = gather_x(ups[1])
    downs.append(gather_x(jnp.where(first, down_got, down_high)))

    flat = lax.optimization_barrier(patches.reshape(patches.shape[0], tokens, -1))
    chosen = order[place[3]]
    piece = lax.dynamic_index_in_dim(flat, chosen, 0, keepdims=False)
    present = lax.dynamic_index_in_dim(field_mask, chosen, 0, keepdims=False)
    present = present.astype(jnp.bfloat16)
    depth = patches.shape[3]
    masked = [piece[:, f * depth : (f + 1) * depth] * present[:, f : f + 1] for f in range(2)]
    message = jnp.concatenate([*masked, jnp.pad(present, ((0, 0), (0, 126)))], axis=1)
    table = embed_weight.reshape(-1, width)
    block = jax.ShapeDtypeStruct((tokens, narrow), jnp.bfloat16)
    partial = jax.ShapeDtypeStruct((tokens, narrow), jnp.float32)
    token = jax.ShapeDtypeStruct((8, 128), jnp.float32)
    starts = [
        (z + RING * xl) * (2 * half) + (core if rel == 0 else 1 - core) * half
        for xl in range(2)
        for rel in range(2)
    ]
    table, bias = (
        jnp.stack([lax.dynamic_slice_in_dim(v, at, half, 1) for at in starts])
        for v in (table, embed_bias)
    )
    operands = [*gather_behind(message, "z"), bias, table]
    *terms, seen = call(
        embed_kernel,
        [block] * RING + [token],
        [place, *operands],
        [SMEM] + [whole(v) for v in operands],
        [
            pltpu.VMEM((RING,) + message.shape, jnp.bfloat16),
            pltpu.VMEM((RING, tokens, narrow), jnp.bfloat16),
        ],
    )
    terms = send_each(terms, "y")

    def add_of(terms, like):
        specs = [whole(t) for t in terms]
        return call(add_kernel, [like, token], terms, specs)

    x, _ = add_of((terms[0], terms[2]), partial)
    x, seen_x = add_of((x, terms[1], terms[3]), block)

    small = tokens // RING
    sent = jax.ShapeDtypeStruct((2 * small, hidden + 128), jnp.bfloat16)
    acted = jax.ShapeDtypeStruct((2 * small, hidden), jnp.bfloat16)

    def up_of(blocks, weights, pair, after=()):
        return call(
            up_kernel,
            [sent] * RING + [token],
            [place, *blocks, *weights],
            [SMEM] + [whole(block)] * 2 + [pair_of(w, pair) for w in weights],
            [pltpu.VMEM((2 * RING, small, hidden + 128), jnp.bfloat16)],
            after,
        )

    def act_of(parts, after=()):
        return call(
            lambda *refs: act_kernel(width, *refs),
            [acted, token],
            parts,
            [whole(sent)] * RING,
            (),
            after,
        )

    def down_of(acts, weights, pair, after=()):
        return call(
            down_kernel,
            [block] * 2 + [token],
            [place, *acts, *weights],
            [SMEM] + [whole(acted)] * RING + [pair_of(w, pair) for w in weights],
            [pltpu.VMEM((2 * RING, small, hidden), jnp.bfloat16)],
            after,
        )

    ready = {}
    for layer in range(4):
        kind, pair = layer % 2, layer // 2
        if pair == 0:
            held = pass_on(ups[kind], seen_x)
            ready["up", kind] = (held, swap_core(held))
        x0, x1, x2, x3 = gather_behind(x, "y")
        *parts, up_a = up_of((x0, x2), ready["up", kind], pair)
        h_a = send_each(parts, "z")
        *parts, up_b = up_of((x1, x3), ready["up", kind], pair, (up_a,))
        h_b = send_each(parts, "z")
        act, seen_a = act_of(h_a, (up_b,))
        acts_a = gather_behind(act, "z")
        act, seen_b = act_of(h_b, (seen_a, acts_a[1], acts_a[3]) if pair == 0 else (seen_a,))
        acts_b = gather_behind(act, "z")
        if pair == 0:
            held = pass_on(downs[kind], seen_b)
            ready["down", kind] = (held, swap_core(held))
        mine, second, down_a = down_of(acts_a, ready["down", kind], pair, (seen_b,))
        second = to_ahead(second, "y", 2)
        first_back, third_back, _ = down_of(acts_b, ready["down", kind], pair, (down_a,))
        first_back = to_ahead(first_back, "y", 3)
        third_back = to_ahead(third_back, "y", 1)
        x, _ = add_of((x, mine, second), partial)
        if layer < 3:
            x, seen_x = add_of((x, first_back, third_back), block)

    out = jax.ShapeDtypeStruct((tokens, 2 * half), jnp.bfloat16)
    last = [x, first_back, third_back]
    one, two = call(last_kernel, [out, out], [place, *last], [SMEM] + [whole(v) for v in last])
    one = grid_move(
        one, lambda a, b: (b // 2 if b % 2 == 0 else 2 + b // 2, a)
    )
    two = grid_move(
        two, lambda a, b: (2 + b // 2 if b % 2 == 0 else b // 2, a)
    )
    front = y < 2
    out = jnp.concatenate([jnp.where(front, one, two), jnp.where(front, two, one)], axis=1)
    return out[None]


def solution(mesh):
    inner = Mesh(mesh.devices.reshape(SIZES), AXES)
    section, field, dp = ("xh", "core"), "y", ("xl", "z")
    in_specs = (
        P(None, dp, field, None),
        P(None, dp, field),
        P(),
        P(field, None, None),
        P(field, None),
        P(section, None),
        P(section, dp, field),
        P(section, field, dp),
    )
    return jax.shard_map(
        per_device, mesh=inner, in_specs=in_specs, out_specs=P(section, dp, field), check_vma=False
    )
```

```python
import jax
import jax.numpy as jnp
from jax import lax
from jax.experimental import pallas as pl
from jax.experimental.pallas import tpu as pltpu
from jax.sharding import Mesh, PartitionSpec as P

AXES = ("xh", "core", "y", "xl", "z")
SIZES = (2, 2, 4, 2, 4)
RING = 4
EPS = 1e-05
SMEM = pl.BlockSpec(memory_space=pltpu.SMEM)
ANY = pl.BlockSpec(memory_space=pl.ANY)


def call(kernel, out_shape, operands, specs, scratch=(), after=(), carry=()):
    kept, extra, made = len(operands), len(after) + len(carry), len(out_shape)

    def body(*refs):
        outs = refs[kept + extra :]
        kernel(*refs[:kept], *outs[:made], *outs[made + len(carry) :])

    return pl.pallas_call(
        body,
        grid=(1,),
        out_shape=list(out_shape) + [jax.ShapeDtypeStruct(v.shape, v.dtype) for v in carry],
        in_specs=list(specs) + [whole(v) for v in after] + [ANY] * len(carry),
        out_specs=[whole(v) for v in out_shape] + [ANY] * len(carry),
        scratch_shapes=list(scratch),
        input_output_aliases={kept + len(after) + i: made + i for i in range(len(carry))},
        compiler_params=pltpu.CompilerParams(vmem_limit_bytes=16 * 2**20),
        cost_estimate=pl.CostEstimate(flops=0, bytes_accessed=0, transcendentals=0),
    )(*operands, *after, *carry)


def whole(like):
    return pl.BlockSpec(like.shape, lambda _: (0,) * len(like.shape))


def pair_of(like, pair):
    return pl.BlockSpec((2,) + like.shape[1:], lambda _: (pair,) + (0,) * (len(like.shape) - 1))


def pass_on(array, after):
    def body(*refs):
        pass

    return pl.pallas_call(
        body,
        out_shape=jax.ShapeDtypeStruct(array.shape, array.dtype),
        grid=(1,),
        in_specs=[ANY, whole(after)],
        out_specs=ANY,
        input_output_aliases={0: 0},
    )(array, after)


def embed_kernel(place, m0, m1, m2, m3, bias, table, *rest):
    outs, token, held, made = rest[:RING], *rest[RING:]
    token[...] = jnp.zeros(token.shape, token.dtype)
    y, z = place[1], place[2]
    depth, half = table.shape[1:]
    for behind, block in enumerate((m0, m1, m2, m3)):
        held[lax.rem(z + RING - behind, RING)] = block[...]
    rows = RING * m0.shape[0]
    pieces = held[...].reshape(rows, held.shape[2])
    present = pieces[:, depth : depth + 128].astype(jnp.float32)
    for k in range(4):
        total = jnp.dot(pieces[:, :depth], table[k], preferred_element_type=jnp.float32)
        for f in range(2):
            total += present[:, f : f + 1] * bias[k, f : f + 1].astype(jnp.float32)
        total = total.astype(jnp.bfloat16).reshape(RING, rows // RING, half)
        made[:, :, k * half : (k + 1) * half] = total
    for ahead in range(RING):
        outs[ahead][...] = made[lax.rem(y + ahead, RING)]


def up_kernel(place, first, second, own, other, *rest):
    outs, token, made = rest[:RING], *rest[RING:]
    token[...] = jnp.zeros(token.shape, token.dtype)
    z = place[2]
    tokens, hidden, half = first.shape[0], own.shape[2], own.shape[1]
    rows, small = 2 * tokens, tokens // RING
    x = jnp.concatenate([first[...], second[...]], axis=0)
    for start in range(0, hidden, 256):
        wide = min(256, hidden - start)
        at = slice(start, start + wide)
        total = jnp.zeros((rows, wide), jnp.float32)
        for xl in range(2):
            for rel, part in enumerate((own, other)):
                k = (xl * 2 + rel) * half
                total += jnp.dot(
                    x[:, k : k + half], part[xl, :, at], preferred_element_type=jnp.float32
                )
        made[:, :, at] = total.astype(jnp.bfloat16).reshape(2 * RING, small, wide)
    values = x.astype(jnp.float32)
    square = jnp.sum(values * values, axis=1, keepdims=True)
    high = square.astype(jnp.bfloat16).astype(jnp.float32)
    lane = lax.broadcasted_iota(jnp.int32, (rows, 128), 1)
    tail = jnp.where(lane == 0, high, jnp.where(lane == 1, square - high, 0.0))
    made[:, :, hidden:] = tail.astype(jnp.bfloat16).reshape(2 * RING, small, 128)
    for ahead in range(RING):
        part = lax.rem(z + ahead, RING)
        outs[ahead][:small] = made[part]
        outs[ahead][small:] = made[RING + part]


def act_kernel(width, h0, h1, h2, h3, out, token):
    token[...] = jnp.zeros(token.shape, token.dtype)
    hidden = out.shape[1]
    blocks = (h0, h1, h2, h3)
    square = jnp.zeros((out.shape[0], 1), jnp.float32)
    for block in blocks:
        tail = block[:, hidden:].astype(jnp.float32)
        square += jnp.sum(tail, axis=1, keepdims=True)
    scale = lax.rsqrt(square / width + EPS)
    total = jnp.zeros(out.shape, jnp.float32)
    for block in blocks:
        total += block[:, :hidden].astype(jnp.float32)
    out[...] = jax.nn.gelu(total * scale, approximate=True).astype(jnp.bfloat16)


def down_kernel(place, a0, a1, a2, a3, own, other, *rest):
    outs, token, held = rest[:2], *rest[2:]
    token[...] = jnp.zeros(token.shape, token.dtype)
    z = place[2]
    small, half = a0.shape[0] // 2, own.shape[2]
    for behind, block in enumerate((a0, a1, a2, a3)):
        part = lax.rem(z + RING - behind, RING)
        held[part] = block[:small]
        held[RING + part] = block[small:]
    tokens = RING * small
    act = held[...].reshape(2 * tokens, held.shape[2])
    for xl in range(2):
        for rel, part in enumerate((own, other)):
            k = (xl * 2 + rel) * half
            total = jnp.dot(act, part[xl], preferred_element_type=jnp.float32)
            total = total.astype(jnp.bfloat16)
            outs[0][:, k : k + half] = total[:tokens]
            outs[1][:, k : k + half] = total[tokens:]


def add_kernel(*refs):
    *terms, out, token = refs
    token[...] = jnp.zeros(token.shape, token.dtype)
    out[...] = sum(t[...].astype(jnp.float32) for t in terms).astype(out.dtype)


def last_kernel(place, part, first, second, one, two):
    total = sum(t[...].astype(jnp.float32) for t in (part, first, second)).astype(jnp.bfloat16)
    half = total.shape[1] // 4
    odd = lax.rem(place[2], 2)
    for xl in range(2):
        for rel in range(2):
            k = (xl * 2 + rel) * half
            piece = total[:, k : k + half]
            side = place[0] if rel == 0 else 1 - place[0]
            at = pl.ds(pl.multiple_of(side * half, half), half)

            @pl.when(odd == xl)
            def _():
                one[:, at] = piece

            @pl.when(odd != xl)
            def _():
                two[:, at] = piece


def to_ahead(block, axis, distance):
    return lax.ppermute(block, axis, [(i, (i + distance) % RING) for i in range(RING)])


def send_each(blocks, axis):
    moved = {d: to_ahead(blocks[d], axis, d) for d in (2, 1, 3)}
    return [blocks[0], moved[1], moved[2], moved[3]]


def gather_behind(block, axis):
    return send_each([block] * RING, axis)


def gather_x(block):
    return lax.all_gather(block, ("xh", "xl"), axis=0, tiled=False)


def swap_core(block):
    return lax.ppermute(block, "core", [(0, 1), (1, 0)])


def grid_move(block, target):
    route = [
        (y * RING + z, target(y, z)[0] * RING + target(y, z)[1])
        for y in range(RING)
        for z in range(RING)
    ]
    return lax.ppermute(block, ("y", "z"), route)


def per_device(patches, field_mask, order, embed_weight, embed_bias, norm_gain, w_up, w_down):
    xh, core, y, xl, z = (lax.axis_index(name) for name in AXES)
    first = core == 0
    tokens = patches.shape[1]
    width = embed_weight.shape[2]
    rows_up = w_up.shape[1]
    hidden = w_up.shape[2]
    half = rows_up // 2
    narrow = width // RING
    place = jnp.stack([core, y, z, 2 * xh + core]).astype(jnp.int32)

    gain = lax.dynamic_slice(norm_gain[0], ((xl * RING + z) * rows_up,), (rows_up,))
    up = (w_up[0].astype(jnp.float32) * gain[:, None]).astype(jnp.bfloat16)
    down = w_down[0]
    up_low, up_high = up[:half], up[half:]
    up_got = swap_core(jnp.where(first, up_high, up_low))
    ups = [gather_x(jnp.where(first, up_low, up_got)), jnp.where(first, up_got, up_high)]

    down_low, down_high = down[:, :half], down[:, half:]
    down_got = swap_core(jnp.where(first, down_high, down_low))
    downs = [gather_x(jnp.where(first, down_low, down_got))]
    ups[1] = gather_x(ups[1])
    downs.append(gather_x(jnp.where(first, down_got, down_high)))

    flat = lax.optimization_barrier(patches.reshape(patches.shape[0], tokens, -1))
    chosen = order[place[3]]
    piece = lax.dynamic_index_in_dim(flat, chosen, 0, keepdims=False)
    present = lax.dynamic_index_in_dim(field_mask, chosen, 0, keepdims=False)
    present = present.astype(jnp.bfloat16)
    depth = patches.shape[3]
    masked = [piece[:, f * depth : (f + 1) * depth] * present[:, f : f + 1] for f in range(2)]
    message = jnp.concatenate([*masked, jnp.pad(present, ((0, 0), (0, 126)))], axis=1)
    table = embed_weight.reshape(-1, width)
    block = jax.ShapeDtypeStruct((tokens, narrow), jnp.bfloat16)
    partial = jax.ShapeDtypeStruct((tokens, narrow), jnp.float32)
    token = jax.ShapeDtypeStruct((8, 128), jnp.float32)
    starts = [
        (z + RING * xl) * (2 * half) + (core if rel == 0 else 1 - core) * half
        for xl in range(2)
        for rel in range(2)
    ]
    table, bias = (
        jnp.stack([lax.dynamic_slice_in_dim(v, at, half, 1) for at in starts])
        for v in (table, embed_bias)
    )
    operands = [*gather_behind(message, "z"), bias, table]
    *terms, seen = call(
        embed_kernel,
        [block] * RING + [token],
        [place, *operands],
        [SMEM] + [whole(v) for v in operands],
        [
            pltpu.VMEM((RING,) + message.shape, jnp.bfloat16),
            pltpu.VMEM((RING, tokens, narrow), jnp.bfloat16),
        ],
    )
    terms = send_each(terms, "y")

    def add_of(terms, like):
        specs = [whole(t) for t in terms]
        return call(add_kernel, [like, token], terms, specs)

    x, _ = add_of((terms[0], terms[2]), partial)
    x, seen_x = add_of((x, terms[1], terms[3]), block)

    small = tokens // RING
    sent = jax.ShapeDtypeStruct((2 * small, hidden + 128), jnp.bfloat16)
    acted = jax.ShapeDtypeStruct((2 * small, hidden), jnp.bfloat16)

    def up_of(blocks, weights, pair, after=()):
        return call(
            up_kernel,
            [sent] * RING + [token],
            [place, *blocks, *weights],
            [SMEM] + [whole(block)] * 2 + [pair_of(w, pair) for w in weights],
            [pltpu.VMEM((2 * RING, small, hidden + 128), jnp.bfloat16)],
            after,
        )

    def act_of(parts, after=(), carry=()):
        return call(
            lambda *refs: act_kernel(width, *refs),
            [acted, token],
            parts,
            [whole(sent)] * RING,
            (),
            after,
            carry,
        )

    def down_of(acts, weights, pair, after=()):
        return call(
            down_kernel,
            [block] * 2 + [token],
            [place, *acts, *weights],
            [SMEM] + [whole(acted)] * RING + [pair_of(w, pair) for w in weights],
            [pltpu.VMEM((2 * RING, small, hidden), jnp.bfloat16)],
            after,
        )

    ready = {}
    for layer in range(4):
        kind, pair = layer % 2, layer // 2
        if pair == 0:
            held = pass_on(ups[kind], seen_x)
            ready["up", kind] = (held, swap_core(held))
        x0, x1, x2, x3 = gather_behind(x, "y")
        *parts, up_a = up_of((x0, x2), ready["up", kind], pair)
        h_a = send_each(parts, "z")
        *parts, up_b = up_of((x1, x3), ready["up", kind], pair, (up_a,))
        h_b = send_each(parts, "z")
        act, seen_a = act_of(h_a, (up_b,))
        acts_a = gather_behind(act, "z")
        if pair == 0:
            act, seen_b, held = act_of(h_b, (seen_a, acts_a[1], acts_a[3]), (downs[kind],))
            ready["down", kind] = (held, swap_core(held))
        else:
            act, seen_b = act_of(h_b, (seen_a,))
        acts_b = gather_behind(act, "z")
        mine, second, down_a = down_of(acts_a, ready["down", kind], pair, (seen_b,))
        second = to_ahead(second, "y", 2)
        first_back, third_back, _ = down_of(acts_b, ready["down", kind], pair, (down_a,))
        first_back = to_ahead(first_back, "y", 3)
        third_back = to_ahead(third_back, "y", 1)
        x, _ = add_of((x, mine, second), partial)
        if layer < 3:
            x, seen_x = add_of((x, first_back, third_back), block)

    out = jax.ShapeDtypeStruct((tokens, 2 * half), jnp.bfloat16)
    last = [x, first_back, third_back]
    one, two = call(last_kernel, [out, out], [place, *last], [SMEM] + [whole(v) for v in last])
    one = grid_move(
        one, lambda a, b: (b // 2 if b % 2 == 0 else 2 + b // 2, a)
    )
    two = grid_move(
        two, lambda a, b: (2 + b // 2 if b % 2 == 0 else b // 2, a)
    )
    front = y < 2
    out = jnp.concatenate([jnp.where(front, one, two), jnp.where(front, two, one)], axis=1)
    return out[None]


def solution(mesh):
    inner = Mesh(mesh.devices.reshape(SIZES), AXES)
    section, field, dp = ("xh", "core"), "y", ("xl", "z")
    in_specs = (
        P(None, dp, field, None),
        P(None, dp, field),
        P(),
        P(field, None, None),
        P(field, None),
        P(section, None),
        P(section, dp, field),
        P(section, field, dp),
    )
    return jax.shard_map(
        per_device, mesh=inner, in_specs=in_specs, out_specs=P(section, dp, field), check_vma=False
    )
```
